32 devices in a mesh: section: 2 (over core), ctx: 4 (over z), dp: 4 (over y, x).
Axes of the slice: x: 2, y: 2, z: 4, core: 2. Of those that a mesh axis runs over, the one named last changes fastest.
Arguments:
- block_input: bfloat16 [2, 8, 1024, 1024], P('section', 'dp', 'ctx'), may hold values from -6 to 6
- out_grad: bfloat16 [2, 8, 1024, 1024], P('section', 'dp', 'ctx'), may hold values from -6 to 6
- segments: int32 [2, 8, 1024], P(None, 'dp'), may hold values from 0 to 4, as said below
- mixer_gain: bfloat16 [2, 1024], P('section', ('ctx', 'dp')), may hold values from 0.5 to 1.5
- mixer_in: bfloat16 [2, 1024, 3328], P('section', ('ctx', 'dp')), may hold values from -0.1875 to 0.1875
- step_proj: bfloat16 [2, 1024, 24], P('section', ('ctx', 'dp')), may hold values from -0.1875 to 0.1875
- step_bias: float32 [2, 24], P('section'), may hold values from -7 to -4
- decay_log: float32 [2, 24], P('section'), may hold values from -1.5 to 1.5
- skip_gain: float32 [2, 24], P('section'), may hold values from 0.5 to 1.5
- conv_taps: bfloat16 [2, 4, 1792], P('section', None, ('ctx', 'dp')), may hold values from -3 to 3
- conv_bias: bfloat16 [2, 1792], P('section', ('ctx', 'dp')), may hold values from -0.5 to 0.5
- gated_gain: bfloat16 [2, 1536], P('section', ('ctx', 'dp')), may hold values from 0.5 to 1.5
- ssm_out: bfloat16 [2, 1536, 1024], P('section', ('ctx', 'dp')), may hold values from -0.15625 to 0.15625
- qkv_proj: bfloat16 [2, 1024, 768], P('section', ('ctx', 'dp')), may hold values from -0.1875 to 0.1875
- attn_out: bfloat16 [2, 512, 1024], P('section', ('ctx', 'dp')), may hold values from -1.5 to 1.5
- ffn_gain: bfloat16 [2, 1024], P('section', ('ctx', 'dp')), may hold values from 0.5 to 1.5
- gate_up: bfloat16 [2, 1024, 4096], P('section', ('ctx', 'dp')), may hold values from -0.1875 to 0.1875
- ffn_down: bfloat16 [2, 2048, 1024], P('section', ('ctx', 'dp')), may hold values from -0.125 to 0.125
Outputs:
- block_output: bfloat16 [2, 8, 1024, 1024], P('section', 'dp', 'ctx')
- input_grad: bfloat16 [2, 8, 1024, 1024], P('section', 'dp', 'ctx')
- mixer_gain_grad: float32 [2, 1024], P('section', ('ctx', 'dp'))
- mixer_in_grad: float32 [2, 1024, 3328], P('section', ('ctx', 'dp'))
- step_proj_grad: float32 [2, 1024, 24], P('section', ('ctx', 'dp'))
- step_bias_grad: float32 [2, 24], P('section')
- decay_log_grad: float32 [2, 24], P('section')
- skip_gain_grad: float32 [2, 24], P('section')
- conv_taps_grad: float32 [2, 4, 1792], P('section', None, ('ctx', 'dp'))
- conv_bias_grad: float32 [2, 1792], P('section', ('ctx', 'dp'))
- gated_gain_grad: float32 [2, 1536], P('section', ('ctx', 'dp'))
- ssm_out_grad: float32 [2, 1536, 1024], P('section', ('ctx', 'dp'))
- qkv_proj_grad: float32 [2, 1024, 768], P('section', ('ctx', 'dp'))
- attn_out_grad: float32 [2, 512, 1024], P('section', ('ctx', 'dp'))
- ffn_gain_grad: float32 [2, 1024], P('section', ('ctx', 'dp'))
- gate_up_grad: float32 [2, 1024, 4096], P('section', ('ctx', 'dp'))
- ffn_down_grad: float32 [2, 2048, 1024], P('section', ('ctx', 'dp'))
The draws below stay inside these ranges and needn't reach their ends.
Inputs may be any that keep to these rules, and one draw needn't show every extreme that they name: `segments`: along each row the document numbers start at 0 and never fall, rising by at most one from a position to the next; in every micro-batch, one row of each aligned block of 2 rows, drawn from the seed, holds a single document, and every other row holds exactly five documents.
All inputs are finite; a program needn't handle non-finite values.
Results may differ from the reference program's by a relative error of at most 0.025.
Values may be sent and summed in bfloat16 or wider, within the bound.
A program may use at most 448 MiB of HBM per device.

```python
import jax
import jax.numpy as jnp
from jax import lax

D = 1024
FF = 2048
HEADS_SSM = 24
HEAD = 64
STATE = 128
CONV = 4
QHEADS = 8
KVHEADS = 2
ROWS_DEV = 2
MICRO = 2
SECTIONS = 2
ROWS = 8
SEQ = 1024


def draw_segments(key, part):
    key = jax.random.fold_in(key, 7)
    cut_key, row_key = jax.random.split(key)
    row_keys = jax.random.split(cut_key, MICRO * ROWS)
    cut_spots = jax.vmap(lambda row_seed: jax.random.permutation(row_seed, SEQ - 1)[:4])(row_keys) + 1
    cut_spots = cut_spots.reshape(MICRO, ROWS, 4)
    position = jnp.arange(SEQ)[None, None, :, None]
    chosen = jax.random.randint(row_key, (MICRO, ROWS // ROWS_DEV), 0, ROWS_DEV)
    single = jnp.repeat(chosen, ROWS_DEV, axis=1) == (jnp.arange(ROWS) % ROWS_DEV)[None, :]
    boundary = jnp.any(position == cut_spots[:, :, None, :], axis=3) & jnp.logical_not(single)[:, :, None]
    return jnp.cumsum(boundary.astype(jnp.int32), axis=2).astype(jnp.int32)


def shard_levels(own_key, shape, cuts, low, largest):
    factor_of = 1.0
    for dim, parts in cuts:
        draws = jax.random.uniform(jax.random.fold_in(jax.random.fold_in(own_key, 6), dim), (parts,), jnp.float32, low / len(cuts), largest / len(cuts))
        factor_of = factor_of * jnp.repeat(jnp.exp(draws), shape[dim] // parts).reshape((-1,) + (1,) * (len(shape) - 1 - dim))
    return factor_of


def scatter_about(stream_key, shape, scale, most, pieces=(), kind=jnp.bfloat16):
    values = jax.random.normal(stream_key, shape, jnp.float32) * scale
    if len(pieces) > 0:
        values = shard_levels(stream_key, shape, pieces, -0.22, 0.18) * values
    return jnp.clip(values, min=-most, max=most).astype(kind)


def setup_inputs(seed: int = 0) -> dict:
    splits = jax.random.split(jax.random.key(seed), 19)
    return {
        "block_input": scatter_about(splits[0], (MICRO, ROWS, SEQ, D), 1.0, 6.0, ((0, 2), (1, 4), (2, 4))),
        "out_grad": scatter_about(splits[1], (MICRO, ROWS, SEQ, D), 1.0, 6.0, ((0, 2), (1, 4), (2, 4))),
        "segments": draw_segments(jax.random.fold_in(splits[18], 71), 0),
        "mixer_gain": jnp.clip(1.0 + 0.1 * jax.random.normal(splits[3], (SECTIONS, D), jnp.float32), 0.5, 1.5).astype(jnp.bfloat16),
        "mixer_in": scatter_about(splits[4], (SECTIONS, D, 2 * HEADS_SSM * HEAD + 2 * STATE), D ** -0.5, 0.1875, ((0, 2), (1, 16))),
        "step_proj": scatter_about(splits[5], (SECTIONS, D, HEADS_SSM), D ** -0.5, 0.1875, ((0, 2), (1, 16))),
        "step_bias": jnp.clip(-7.0 + 3.0 * jax.random.uniform(splits[6], (SECTIONS, HEADS_SSM), jnp.float32) ** shard_levels(splits[6], (SECTIONS, HEADS_SSM), ((0, 2),), -0.2, 0.2), -7.0, -4.0),
        "decay_log": jnp.clip(jax.random.uniform(splits[7], (SECTIONS, HEADS_SSM), jnp.float32, -1.5, 1.5) * shard_levels(splits[7], (SECTIONS, HEADS_SSM), ((0, 2),), -0.4, 0.0), -1.5, 1.5),
        "skip_gain": jnp.clip(0.5 + 1.0 * jax.random.uniform(splits[8], (SECTIONS, HEADS_SSM), jnp.float32) ** shard_levels(splits[8], (SECTIONS, HEADS_SSM), ((0, 2),), -0.2, 0.2), 0.5, 1.5),
        "conv_taps": scatter_about(splits[9], (SECTIONS, CONV, HEADS_SSM * HEAD + 2 * STATE), CONV ** -0.5, 3.0, ((0, 2), (2, 16))),
        "conv_bias": jnp.clip(jax.random.uniform(splits[10], (SECTIONS, HEADS_SSM * HEAD + 2 * STATE), jnp.float32, -0.5, 0.5) * shard_levels(splits[10], (SECTIONS, HEADS_SSM * HEAD + 2 * STATE), ((0, 2), (1, 16)), -0.4, 0.0), -0.5, 0.5).astype(jnp.bfloat16),
        "gated_gain": jnp.clip(1.0 + 0.1 * jax.random.normal(splits[11], (SECTIONS, HEADS_SSM * HEAD), jnp.float32), 0.5, 1.5).astype(jnp.bfloat16),
        "ssm_out": scatter_about(splits[12], (SECTIONS, HEADS_SSM * HEAD, D), (HEADS_SSM * HEAD) ** -0.5, 0.15625, ((0, 2), (1, 16))),
        "qkv_proj": scatter_about(splits[13], (SECTIONS, D, (QHEADS + 2 * KVHEADS) * HEAD), D ** -0.5, 0.1875, ((0, 2), (1, 16))),
        "attn_out": scatter_about(splits[14], (SECTIONS, QHEADS * HEAD, D), (HEAD // 4) ** -0.5, 1.5, ((0, 2), (1, 16))),
        "ffn_gain": jnp.clip(1.0 + 0.1 * jax.random.normal(splits[15], (SECTIONS, D), jnp.float32), 0.5, 1.5).astype(jnp.bfloat16),
        "gate_up": scatter_about(splits[16], (SECTIONS, D, 2 * FF), D ** -0.5, 0.1875, ((0, 2), (1, 16))),
        "ffn_down": scatter_about(splits[17], (SECTIONS, FF, D), FF ** -0.5, 0.125, ((0, 2), (1, 16))),
    }


small_eps = 1e-06
masked_score = -1e+30
rope_base = 10000.0
highest = lax.Precision.HIGHEST

@jax.custom_vjp
def low(v):
    return lax.optimization_barrier(v.astype(jnp.bfloat16)).astype(jnp.float32)

@jax.custom_vjp
def low_back(v):
    return v

def low_keep(v):
    return (low(v), None)

def low_pass(kept, grad):
    return (grad,)

def back_keep(v):
    return (v, None)

def back_low(kept, grad):
    return (low(grad),)
low.defvjp(low_keep, low_pass)
low_back.defvjp(back_keep, back_low)

def rms_scale(values, gain_vec):
    mean_square = lax.optimization_barrier(jnp.mean(values * values, axis=-1, keepdims=True))
    return values * lax.rsqrt(mean_square + small_eps) * gain_vec

def rotate(values, positions):
    half_dim = values.shape[-1] // 2
    frequency = rope_base ** (-jnp.arange(half_dim, dtype=jnp.float32) / half_dim)
    angles = positions.astype(jnp.float32)[:, None] * frequency[None, :]
    cosine = jnp.cos(angles)[:, None, :]
    sine_part = jnp.sin(angles)[:, None, :]
    first_half = values[..., :half_dim]
    second_half = values[..., half_dim:]
    return jnp.concatenate([first_half * cosine - second_half * sine_part, second_half * cosine + first_half * sine_part], axis=-1)

def conv_mix(extended, kernel, shift_bias, seg_ext):
    lag_count = kernel.shape[0]
    span_len = extended.shape[1] - lag_count + 1
    summed = shift_bias + jnp.zeros((extended.shape[0], span_len, extended.shape[2]), extended.dtype)
    for lag_index in range(lag_count):
        same_doc = seg_ext[:, lag_index:lag_index + span_len] == seg_ext[:, lag_count - 1:]
        summed = summed + kernel[lag_index] * extended[:, lag_index:lag_index + span_len] * same_doc[..., None].astype(extended.dtype)
    return jax.nn.silu(summed)

def step_sizes(dt_heads, step_bias, decay_log):
    step_size = jax.nn.softplus(dt_heads + step_bias)
    return (step_size, step_size * -jnp.exp(decay_log))

def block_mix(ssm_input, write_proj, read_proj, dt_heads, step_bias, decay_log, skip_gain, state_in, seg_piece, seg_prev):
    step_size, log_decay = step_sizes(dt_heads, step_bias, decay_log)
    cumulated = jnp.cumsum(log_decay, axis=1)
    span_len = ssm_input.shape[1]
    order_idx = jnp.arange(span_len)
    causal = order_idx[:, None] >= order_idx[None, :]
    same_doc = (seg_piece[:, :, None] == seg_piece[:, None, :]) & causal[None]
    gap_log = jnp.where(same_doc[..., None], cumulated[:, :, None, :] - cumulated[:, None, :, :], masked_score)
    intersection = jnp.einsum('rtn,rsn->rts', read_proj, write_proj, precision=highest)
    mixing = jnp.exp(gap_log) * intersection[..., None] * step_size[:, None, :, :]
    result = jnp.einsum('rtsh,rshe->rthe', mixing, ssm_input, precision=highest)
    carry_in = jnp.exp(cumulated) * (seg_piece == seg_prev[:, None]).astype(log_decay.dtype)[..., None]
    result = result + jnp.einsum('rtn,rhne->rthe', read_proj, state_in, precision=highest) * carry_in[..., None]
    result = result + skip_gain[:, None] * ssm_input
    return result.reshape(result.shape[0], span_len, -1)

def gated_norm(values, gate_vals, gain_vec):
    return rms_scale(values * jax.nn.silu(gate_vals), gain_vec)

def project(left_op, right_op):
    return jnp.dot(left_op, right_op, precision=highest)

def layer_apply(hidden, params, doc_ids):
    mixer_gain, mixer_in, step_proj, step_bias, decay_log, skip_gain, conv_taps, conv_bias, gated_gain, ssm_out, qkv_proj, attn_out, ffn_gain, gate_up, ffn_down = params
    length = hidden.shape[0]
    inner_width = HEADS_SSM * HEAD
    q_width = QHEADS * HEAD
    kv_width = KVHEADS * HEAD
    normed = low(rms_scale(hidden, mixer_gain))
    mixed_in = low_back(project(normed, mixer_in))
    dt_raw = low_back(project(normed, step_proj))
    triple = low_back(project(normed, qkv_proj))
    gate_z = mixed_in[:, :inner_width]
    conv_in = low(mixed_in[:, inner_width:])
    seg_row = doc_ids[None]
    extended = jnp.pad(conv_in, ((CONV - 1, 0), (0, 0)))[None]
    seg_ext = jnp.pad(seg_row, ((0, 0), (CONV - 1, 0)), constant_values=-1)
    conv_out = conv_mix(extended, conv_taps, conv_bias, seg_ext)
    ssm_input = conv_out[..., :inner_width].reshape(1, length, HEADS_SSM, HEAD)
    write_proj = conv_out[..., inner_width:inner_width + STATE]
    read_proj = conv_out[..., inner_width + STATE:]
    dt_heads = dt_raw.reshape(1, length, HEADS_SSM)
    state_in = jnp.zeros((1, HEADS_SSM, STATE, HEAD), jnp.float32)
    seg_prev = jnp.full((1,), -1, jnp.int32)
    ssm_output = block_mix(ssm_input, write_proj, read_proj, dt_heads, step_bias, decay_log, skip_gain, state_in, seg_row, seg_prev)[0]
    gated_out = low(gated_norm(ssm_output, gate_z, gated_gain))
    mamba_out = low_back(project(gated_out, ssm_out))
    positions = jnp.arange(length)
    queries = low(rotate(triple[:, :q_width].reshape(length, QHEADS, HEAD), positions))
    key_rows = low(rotate(triple[:, q_width:q_width + kv_width].reshape(length, KVHEADS, HEAD), positions))
    value_rows = low(triple[:, q_width + kv_width:]).reshape(length, KVHEADS, HEAD)
    grouped = queries.reshape(length, KVHEADS, QHEADS // KVHEADS, HEAD)
    raw_scores = low_back(jnp.einsum('qgid,sgd->giqs', grouped, key_rows, precision=highest) * HEAD ** (-0.5))
    causal = positions[:, None] >= positions[None, :]
    same_doc = doc_ids[:, None] == doc_ids[None, :]
    scores = jnp.where((causal & same_doc)[None, None], raw_scores, masked_score)
    row_max = lax.optimization_barrier(jnp.max(scores, axis=-1, keepdims=True))
    exp_scores = jnp.exp(scores - row_max)
    attn_probs = low(exp_scores / lax.optimization_barrier(jnp.sum(exp_scores, axis=-1, keepdims=True)))
    context = low(low_back(jnp.einsum('giqs,sgd->qgid', attn_probs, value_rows, precision=highest)))
    attn_part = low_back(project(context.reshape(length, q_width), attn_out))
    settled = hidden + mamba_out + attn_part
    ffn_in = low(rms_scale(settled, ffn_gain))
    gate_up_out = low_back(project(ffn_in, gate_up))
    activated = low(jax.nn.silu(gate_up_out[:, :FF]) * gate_up_out[:, FF:])
    return settled + low_back(project(activated, ffn_down))

def reference(block_input, out_grad, segments, mixer_gain, mixer_in, step_proj, step_bias, decay_log, skip_gain, conv_taps, conv_bias, gated_gain, ssm_out, qkv_proj, attn_out, ffn_gain, gate_up, ffn_down):
    weights = (mixer_gain, mixer_in, step_proj, step_bias, decay_log, skip_gain, conv_taps, conv_bias, gated_gain, ssm_out, qkv_proj, attn_out, ffn_gain, gate_up, ffn_down)
    floats = tuple((weight_arr.astype(jnp.float32) for weight_arr in weights))
    first_params = tuple((weight_arr[0] for weight_arr in floats))
    second_params = tuple((weight_arr[1] for weight_arr in floats))

    def two_layers(layer_input, first_set, second_set, doc_ids):
        layer_input = low_back(layer_input)
        middle = low_back(low(layer_apply(layer_input, first_set, doc_ids)))
        return layer_apply(middle, second_set, doc_ids)

    def per_sequence(grad_totals, sequence_item):
        layer_input, cotangent, doc_ids = sequence_item
        result, pullback = jax.vjp(lambda entry_vals, first_set, second_set: two_layers(entry_vals, first_set, second_set, doc_ids), layer_input.astype(jnp.float32), first_params, second_params)
        grad_entry, grad_first, grad_second = pullback(cotangent.astype(jnp.float32))
        grad_totals = jax.tree.map(lambda total_arr, left_leaf, right_leaf: total_arr + jnp.stack([left_leaf, right_leaf]), grad_totals, grad_first, grad_second)
        return (grad_totals, (result.astype(jnp.bfloat16), grad_entry.astype(jnp.bfloat16)))
    flat_items = (block_input.reshape(-1, SEQ, D), out_grad.reshape(-1, SEQ, D), segments.reshape(-1, SEQ))
    zero_totals = tuple((jnp.zeros(weight_arr.shape, jnp.float32) for weight_arr in weights))
    totals, (outputs, entry_grads) = lax.scan(per_sequence, zero_totals, flat_items)
    return (outputs.reshape(block_input.shape), entry_grads.reshape(block_input.shape), totals[0], totals[1], totals[2], totals[3], totals[4], totals[5], totals[6], totals[7], totals[8], totals[9], totals[10], totals[11], totals[12], totals[13], totals[14])
```

```python
import jax
import jax.numpy as jnp
from jax import lax
from jax.sharding import PartitionSpec as P

HEADS_SSM = 24
HEAD = 64
STATE = 128
CONV = 4
QHEADS = 8
KVHEADS = 2


small_eps = 1e-06
masked_score = -1e30
rope_base = 10000.0
highest = lax.Precision.HIGHEST


def from_behind(array, axis, by):
    peers = lax.axis_size(axis)
    pairs = [(i, i + by) for i in range(peers) if 0 <= i + by < peers]
    return lax.ppermute(array, axis, pairs)


def gathered_states(decays, states):
    return (
        lax.all_gather(decays.astype(jnp.bfloat16), "ctx"),
        lax.all_gather(states.astype(jnp.bfloat16), "ctx"),
    )


def joined(gathered, order, used):
    decays, states = gathered
    total = jnp.zeros(states.shape[1:], jnp.float32)
    for source in order:
        decay = jnp.where(used(source), decays[source].astype(jnp.float32), 1.0)
        state = jnp.where(used(source), states[source].astype(jnp.float32), 0.0)
        total = total * decay[:, None, :, None] + state
    return total


def prefix(decays, states):
    place = lax.axis_index("ctx")
    count = lax.axis_size("ctx")
    return joined(gathered_states(decays, states), range(count), lambda j: j < place)


def suffix(decays, states):
    place = lax.axis_index("ctx")
    count = lax.axis_size("ctx")
    return joined(gathered_states(decays, states), range(count - 1, -1, -1), lambda j: j > place)


def for_sending(array):

    def short(part):
        return part.astype(jnp.bfloat16) if part.dtype == jnp.float32 else part

    return jax.tree.map(short, array)


def swapped(value, axis, stride):
    mask = 2**stride
    pairs = [(source, source ^ mask) for source in range(lax.axis_size(axis))]
    return lax.ppermute(value, axis, pairs)


def rms_scale(values, gain_vec):
    mean_square = jnp.mean(values * values, axis=-1, keepdims=True)
    return values * lax.rsqrt(mean_square + small_eps) * gain_vec


def rotate(values, positions):
    half_dim = values.shape[-1] // 2
    frequency = rope_base ** (-jnp.arange(half_dim, dtype=jnp.float32) / half_dim)
    angles = positions.astype(jnp.float32)[:, None] * frequency[None, :]
    cosine = jnp.cos(angles)[:, None, :]
    sine_part = jnp.sin(angles)[:, None, :]
    first_half = values[..., :half_dim]
    second_half = values[..., half_dim:]
    return jnp.concatenate(
        [
            first_half * cosine - second_half * sine_part,
            second_half * cosine + first_half * sine_part,
        ],
        axis=-1,
    )


def conv_mix(extended, kernel, shift_bias, seg_ext):
    lag_count = kernel.shape[0]
    span_len = extended.shape[1] - lag_count + 1
    summed = shift_bias + jnp.zeros(
        (extended.shape[0], span_len, extended.shape[2]), extended.dtype
    )
    for lag_index in range(lag_count):
        same_doc = seg_ext[:, lag_index : lag_index + span_len] == seg_ext[:, lag_count - 1 :]
        summed = summed + kernel[lag_index] * extended[
            :, lag_index : lag_index + span_len
        ] * same_doc[..., None].astype(extended.dtype)
    return jax.nn.silu(summed)


def step_sizes(dt_heads, step_bias, decay_log):
    step_size = jax.nn.softplus(dt_heads + step_bias)
    log_decay = step_size * -jnp.exp(decay_log)
    span_len = dt_heads.shape[1]
    order_idx = jnp.arange(span_len)
    lower = (order_idx[:, None] >= order_idx[None, :]).astype(jnp.float32)
    cumulated = jnp.einsum("ts,rsh->rth", lower, log_decay, precision=highest)
    return (step_size, cumulated)


def over_features(per_head):
    owner = jnp.arange(HEADS_SSM * HEAD) // HEAD
    spread = (jnp.arange(HEADS_SSM)[:, None] == owner[None, :]).astype(jnp.float32)
    return jnp.einsum("rth,hf->rtf", per_head, spread, precision=highest)


def block_state(ssm_input, write_proj, dt_heads, step_bias, decay_log, seg_piece, seg_prev):
    step_size, cumulated = step_sizes(dt_heads, step_bias, decay_log)
    piece_total = cumulated[:, -1]
    at_end = (seg_piece == seg_piece[:, -1:]).astype(jnp.float32)
    weight = jnp.exp(piece_total[:, None, :] - cumulated) * step_size * at_end[..., None]
    end_state = jnp.einsum(
        "rpn,rpf->rnf",
        write_proj,
        ssm_input * over_features(weight),
        preferred_element_type=jnp.float32,
    )
    carried = (seg_piece[:, -1] == seg_prev).astype(jnp.float32)
    return (
        jnp.exp(piece_total) * carried[:, None],
        end_state.reshape(end_state.shape[0], STATE, HEADS_SSM, HEAD),
    )


def block_mix(
    ssm_input,
    write_proj,
    read_proj,
    dt_heads,
    step_bias,
    decay_log,
    skip_gain,
    state_in,
    seg_piece,
    seg_prev,
):
    step_size, cumulated = step_sizes(dt_heads, step_bias, decay_log)
    row_count, span_len = ssm_input.shape[:2]
    order_idx = jnp.arange(span_len)
    causal = order_idx[:, None] >= order_idx[None, :]
    same_doc = (seg_piece[:, :, None] == seg_piece[:, None, :]) & causal[None]
    cum_heads = jnp.transpose(cumulated, (0, 2, 1))
    step_heads = jnp.transpose(step_size, (0, 2, 1))
    gap_log = jnp.where(
        same_doc[:, None], cum_heads[:, :, :, None] - cum_heads[:, :, None, :], masked_score
    )
    intersection = jnp.einsum(
        "rtn,rsn->rts", read_proj, write_proj, preferred_element_type=jnp.float32
    )
    mixing = jnp.exp(gap_log) * intersection[:, None] * step_heads[:, :, None, :]
    by_head = ssm_input.reshape(row_count, span_len, HEADS_SSM, HEAD)
    result = jnp.einsum(
        "rhts,rshe->rthe", mixing, by_head, preferred_element_type=jnp.float32
    ).reshape(row_count, span_len, -1)
    carry_in = (
        jnp.exp(cumulated) * (seg_piece == seg_prev[:, None]).astype(jnp.float32)[..., None]
    )
    carried = jnp.einsum(
        "rtn,rnf->rtf",
        read_proj,
        state_in.reshape(row_count, STATE, -1),
        preferred_element_type=jnp.float32,
    )
    result = result + carried * over_features(carry_in)
    return result + jnp.repeat(skip_gain, HEAD) * ssm_input


def gated_norm(values, gate_vals, gain_vec):
    return rms_scale(values * jax.nn.silu(gate_vals), gain_vec)


def attention_mask(seg_piece, seg_rows, offset):
    query_pos = offset + jnp.arange(seg_piece.shape[1])
    causal = query_pos[:, None] >= jnp.arange(seg_rows.shape[1])[None, :]
    same_doc = seg_piece[:, :, None] == seg_rows[:, None, :]
    return (causal[None] & same_doc)[:, None, None]


def scores_of(queries, all_keys, key_mask):
    row_count, piece_size = queries.shape[:2]
    grouped = queries.reshape(row_count, piece_size, KVHEADS, QHEADS // KVHEADS, HEAD)
    keyed = all_keys.reshape(row_count, -1, KVHEADS, HEAD)
    raw_scores = jnp.einsum(
        "rqgid,rsgd->rgiqs", grouped, keyed, preferred_element_type=jnp.float32
    ) * HEAD ** (-0.5)
    return jnp.where(key_mask, raw_scores, masked_score)


def layer_forward(hidden, seg_rows, weights, head_params, ctx_index):
    mixer_gain, step_proj, conv_taps, conv_bias, gated_gain, ffn_gain = weights["small"]
    front = weights["front"]
    ssm_out, attn_out = weights["ssm_out"], weights["attn_out"]
    gate_up, ffn_down = weights["gate_up"], weights["ffn_down"]
    step_bias, decay_log, skip_gain = head_params
    row_count, piece_size, model_width = hidden.shape
    inner_width = HEADS_SSM * HEAD
    q_width = QHEADS * HEAD
    kv_width = KVHEADS * HEAD
    offset = ctx_index * piece_size
    seg_piece = lax.dynamic_slice_in_dim(seg_rows, offset, piece_size, 1)
    seg_pad = jnp.pad(seg_rows, ((0, 0), (CONV - 1, 0)), constant_values=-1)
    seg_ext = lax.dynamic_slice_in_dim(seg_pad, offset, piece_size + CONV - 1, 1)
    seg_prev = seg_ext[:, CONV - 2]
    tokens = hidden.reshape(row_count * piece_size, model_width)
    normed = rms_scale(tokens, mixer_gain.astype(jnp.float32)).astype(jnp.bfloat16)
    fronted = jnp.dot(normed, front, preferred_element_type=jnp.float32)
    qkv_width = q_width + 2 * kv_width
    mixed_in = fronted[:, : front.shape[1] - qkv_width]
    triple = fronted[:, front.shape[1] - qkv_width :]
    dt_raw = jnp.dot(normed, step_proj, preferred_element_type=jnp.float32)
    gate_z = mixed_in[:, :inner_width]
    conv_in = mixed_in[:, inner_width:].astype(jnp.bfloat16).reshape(row_count, piece_size, -1)
    before = from_behind(conv_in[:, piece_size - CONV + 1 :], "ctx", 1)
    extended = jnp.concatenate([before, conv_in], axis=1).astype(jnp.float32)
    conv_out = conv_mix(
        extended, conv_taps.astype(jnp.float32), conv_bias.astype(jnp.float32), seg_ext
    )
    ssm_input = conv_out[..., :inner_width]
    write_proj = conv_out[..., inner_width : inner_width + STATE]
    read_proj = conv_out[..., inner_width + STATE :]
    dt_heads = dt_raw.reshape(row_count, piece_size, HEADS_SSM)
    decays, local_state = block_state(
        ssm_input, write_proj, dt_heads, step_bias, decay_log, seg_piece, seg_prev
    )
    state_in = prefix(decays, local_state)
    ssm_output = block_mix(
        ssm_input,
        write_proj,
        read_proj,
        dt_heads,
        step_bias,
        decay_log,
        skip_gain,
        state_in,
        seg_piece,
        seg_prev,
    ).reshape(row_count * piece_size, inner_width)
    gated_out = gated_norm(ssm_output, gate_z, gated_gain.astype(jnp.float32)).astype(jnp.bfloat16)
    mamba_out = jnp.dot(gated_out, ssm_out, preferred_element_type=jnp.float32)
    positions = offset + jnp.arange(piece_size)
    queries = rotate(
        triple[:, :q_width].reshape(row_count, piece_size, QHEADS, HEAD), positions
    ).astype(jnp.bfloat16)
    key_rows = rotate(
        triple[:, q_width : q_width + kv_width].reshape(row_count, piece_size, KVHEADS, HEAD),
        positions,
    ).astype(jnp.bfloat16)
    value_rows = (
        triple[:, q_width + kv_width :]
        .astype(jnp.bfloat16)
        .reshape(row_count, piece_size, kv_width)
    )
    all_keys, all_values = (
        lax.all_gather(
            key_rows.reshape(row_count, piece_size, kv_width), "ctx", axis=1, tiled=True
        ),
        lax.all_gather(value_rows, "ctx", axis=1, tiled=True),
    )
    key_mask = attention_mask(seg_piece, seg_rows, offset)
    scores = scores_of(queries, all_keys, key_mask)
    row_max = jnp.max(scores, axis=-1, keepdims=True)
    exp_scores = jnp.exp(scores - row_max)
    row_total = jnp.sum(exp_scores, axis=-1, keepdims=True)
    attn_probs = (exp_scores / row_total).astype(jnp.bfloat16)
    log_total = row_max + jnp.log(row_total)
    context = jnp.einsum(
        "rgiqs,rsgd->rqgid",
        attn_probs,
        all_values.reshape(row_count, -1, KVHEADS, HEAD),
        preferred_element_type=jnp.float32,
    )
    context_low = context.reshape(row_count * piece_size, q_width).astype(jnp.bfloat16)
    attn_part = jnp.dot(context_low, attn_out, preferred_element_type=jnp.float32)
    settled = tokens + mamba_out + attn_part
    ffn_in = rms_scale(settled, ffn_gain.astype(jnp.float32)).astype(jnp.bfloat16)
    gate_up_out = jnp.dot(ffn_in, gate_up, preferred_element_type=jnp.float32)
    ff_width = gate_up_out.shape[1] // 2
    activated = (jax.nn.silu(gate_up_out[:, :ff_width]) * gate_up_out[:, ff_width:]).astype(
        jnp.bfloat16
    )
    result = settled + jnp.dot(activated, ffn_down, preferred_element_type=jnp.float32)
    saved = dict(
        tokens=tokens,
        normed=normed,
        gate_z=gate_z,
        extended=extended,
        ssm_input=ssm_input,
        write_proj=write_proj,
        read_proj=read_proj,
        dt_heads=dt_heads,
        decays=decays,
        state_in=state_in,
        ssm_output=ssm_output,
        gated_out=gated_out,
        queries=queries,
        all_keys=all_keys,
        all_values=all_values,
        log_total=log_total,
        context_low=context_low,
        settled=settled,
        ffn_in=ffn_in,
        gate_up_out=gate_up_out,
        activated=activated,
        seg_piece=seg_piece,
        seg_prev=seg_prev,
        seg_ext=seg_ext,
        seg_rows=seg_rows,
        offset=offset,
    )
    return (result.reshape(row_count, piece_size, model_width), saved)


def layer_backward(grad_out, saved, weights, head_params):
    mixer_gain, step_proj, conv_taps, conv_bias, gated_gain, ffn_gain = weights["small"]
    front = weights["front"]
    ssm_out, attn_out = weights["ssm_out"], weights["attn_out"]
    gate_up, ffn_down = weights["gate_up"], weights["ffn_down"]
    step_bias, decay_log, skip_gain = head_params
    row_count, piece_size = saved["dt_heads"].shape[:2]
    tokens = saved["tokens"]
    model_width = tokens.shape[1]
    inner_width = HEADS_SSM * HEAD
    q_width = QHEADS * HEAD
    kv_width = KVHEADS * HEAD
    score_scale = HEAD ** (-0.5)
    seg_piece = saved["seg_piece"]
    seg_prev = saved["seg_prev"]
    seg_ext = saved["seg_ext"]
    grad_flat = grad_out.reshape(-1, model_width)
    grad_low = grad_flat.astype(jnp.bfloat16)
    grad_down = jnp.dot(saved["activated"].T, grad_low, preferred_element_type=jnp.float32)
    grad_act = jnp.dot(grad_low, ffn_down.T, preferred_element_type=jnp.float32)
    gate_up_out = saved["gate_up_out"]
    ff_width = gate_up_out.shape[1] // 2
    gate_part = gate_up_out[:, :ff_width]
    up_part = gate_up_out[:, ff_width:]
    sigmoid_gate = jax.nn.sigmoid(gate_part)
    grad_up = grad_act * gate_part * sigmoid_gate
    grad_gate = grad_act * up_part * sigmoid_gate * (1.0 + gate_part * (1.0 - sigmoid_gate))
    grad_gu = jnp.concatenate([grad_gate, grad_up], axis=1).astype(jnp.bfloat16)
    grad_gate_up = jnp.dot(saved["ffn_in"].T, grad_gu, preferred_element_type=jnp.float32)
    grad_ffn_in = jnp.dot(grad_gu, gate_up.T, preferred_element_type=jnp.float32)
    unused, norm_pull = jax.vjp(rms_scale, saved["settled"], ffn_gain.astype(jnp.float32))
    grad_settled, grad_ffn_gain = norm_pull(grad_ffn_in)
    grad_settled = grad_settled + grad_flat
    settled_low = grad_settled.astype(jnp.bfloat16)
    grad_ssm_out = jnp.dot(saved["gated_out"].T, settled_low, preferred_element_type=jnp.float32)
    grad_gated = jnp.dot(settled_low, ssm_out.T, preferred_element_type=jnp.float32)
    grad_attn_out = jnp.dot(saved["context_low"].T, settled_low, preferred_element_type=jnp.float32)
    grad_context = (
        jnp.dot(settled_low, attn_out.T, preferred_element_type=jnp.float32)
        .astype(jnp.bfloat16)
        .reshape(row_count, piece_size, KVHEADS, QHEADS // KVHEADS, HEAD)
    )
    key_mask = attention_mask(seg_piece, saved["seg_rows"], saved["offset"])
    queries = saved["queries"]
    scores = scores_of(queries, saved["all_keys"], key_mask)
    attn_probs = jnp.exp(scores - saved["log_total"])
    probs_low = attn_probs.astype(jnp.bfloat16)
    value_heads = saved["all_values"].reshape(row_count, -1, KVHEADS, HEAD)
    key_heads = saved["all_keys"].reshape(row_count, -1, KVHEADS, HEAD)
    grad_probs = jnp.einsum(
        "rqgid,rsgd->rgiqs", grad_context, value_heads, preferred_element_type=jnp.float32
    )
    shared = jnp.sum(attn_probs * grad_probs, axis=-1, keepdims=True)
    grad_scores = (attn_probs * (grad_probs - shared)).astype(jnp.bfloat16)
    grouped = queries.reshape(row_count, piece_size, KVHEADS, QHEADS // KVHEADS, HEAD)
    grad_queries = (
        jnp.einsum("rgiqs,rsgd->rqgid", grad_scores, key_heads, preferred_element_type=jnp.float32)
        * score_scale
    )
    row_span = piece_size * lax.axis_size("ctx")
    part_scores = lax.slice_in_dim(grad_scores, 0, row_span, axis=4)
    part_probs = lax.slice_in_dim(probs_low, 0, row_span, axis=4)
    grad_key_part = (
        jnp.einsum("rgiqs,rqgid->srgd", part_scores, grouped, preferred_element_type=jnp.float32)
        * score_scale
    )
    grad_value_part = jnp.einsum(
        "rgiqs,rqgid->srgd", part_probs, grad_context, preferred_element_type=jnp.float32
    )
    key_grads = lax.psum_scatter(
        jnp.concatenate(
            [
                grad_key_part.reshape(row_span, row_count, kv_width),
                grad_value_part.reshape(row_span, row_count, kv_width),
            ],
            axis=2,
        ).astype(jnp.bfloat16),
        "ctx",
        scatter_dimension=0,
        tiled=True,
    ).astype(jnp.float32)
    positions = saved["offset"] + jnp.arange(piece_size)
    grad_key_rows = jnp.transpose(key_grads[..., :kv_width], (1, 0, 2)).reshape(
        row_count, piece_size, KVHEADS, HEAD
    )
    grad_value_rows = jnp.transpose(key_grads[..., kv_width:], (1, 0, 2)).reshape(
        row_count * piece_size, kv_width
    )
    grad_q_pre = rotate(grad_queries.reshape(row_count, piece_size, QHEADS, HEAD), -positions)
    grad_k_pre = rotate(grad_key_rows, -positions)
    grad_triple = jnp.concatenate(
        [grad_q_pre.reshape(-1, q_width), grad_k_pre.reshape(-1, kv_width), grad_value_rows], axis=1
    ).astype(jnp.bfloat16)
    normed = saved["normed"]
    unused, gate_pull = jax.vjp(
        gated_norm, saved["ssm_output"], saved["gate_z"], gated_gain.astype(jnp.float32)
    )
    grad_ssm_output, grad_gate_z, grad_gated_gain = gate_pull(grad_gated)

    def mix_local(
        ssm_input, write_proj, read_proj, dt_heads, bias_vec, log_vec, skip_vec, state_in
    ):
        return block_mix(
            ssm_input,
            write_proj,
            read_proj,
            dt_heads,
            bias_vec,
            log_vec,
            skip_vec,
            state_in,
            seg_piece,
            seg_prev,
        )

    unused, mix_pull = jax.vjp(
        mix_local,
        saved["ssm_input"],
        saved["write_proj"],
        saved["read_proj"],
        saved["dt_heads"],
        step_bias,
        decay_log,
        skip_gain,
        saved["state_in"],
    )
    (
        grad_input_a,
        grad_write_a,
        grad_read,
        grad_dt_a,
        grad_bias_a,
        grad_log_a,
        grad_skip,
        grad_state_in,
    ) = mix_pull(grad_ssm_output.reshape(row_count, piece_size, inner_width))
    decays = saved["decays"]
    state_after = suffix(decays, grad_state_in)
    grad_decays = jnp.sum(state_after * saved["state_in"], axis=(1, 3))

    def state_local(ssm_input, write_proj, dt_heads, bias_vec, log_vec):
        return block_state(ssm_input, write_proj, dt_heads, bias_vec, log_vec, seg_piece, seg_prev)

    unused, state_pull = jax.vjp(
        state_local,
        saved["ssm_input"],
        saved["write_proj"],
        saved["dt_heads"],
        step_bias,
        decay_log,
    )
    grad_input_b, grad_write_b, grad_dt_b, grad_bias_b, grad_log_b = state_pull(
        (grad_decays, state_after)
    )
    grad_conv_out = jnp.concatenate(
        [
            grad_input_a + grad_input_b,
            grad_write_a + grad_write_b,
            grad_read,
        ],
        axis=2,
    )

    def conv_local(extended, kernel, shift_bias):
        return conv_mix(extended, kernel, shift_bias, seg_ext)

    unused, conv_pull = jax.vjp(
        conv_local, saved["extended"], conv_taps.astype(jnp.float32), conv_bias.astype(jnp.float32)
    )
    grad_extended, grad_taps, grad_conv_bias = conv_pull(grad_conv_out)
    spill = CONV - 1
    returned = from_behind(for_sending(grad_extended[:, :spill]), "ctx", -1)
    grad_conv_in = grad_extended[:, spill:] + jnp.pad(
        returned, ((0, 0), (piece_size - spill, 0), (0, 0))
    )
    grad_front_out = jnp.concatenate(
        [
            grad_gate_z.astype(jnp.bfloat16),
            grad_conv_in.reshape(row_count * piece_size, -1).astype(jnp.bfloat16),
            grad_triple,
        ],
        axis=1,
    )
    grad_dt = (
        (grad_dt_a + grad_dt_b).reshape(row_count * piece_size, HEADS_SSM).astype(jnp.bfloat16)
    )
    grad_front = jnp.dot(normed.T, grad_front_out, preferred_element_type=jnp.float32)
    grad_step_proj = jnp.dot(normed.T, grad_dt, preferred_element_type=jnp.float32)
    grad_normed = jnp.dot(grad_front_out, front.T, preferred_element_type=jnp.float32) + jnp.dot(
        grad_dt, step_proj.T, preferred_element_type=jnp.float32
    )
    unused, front_pull = jax.vjp(rms_scale, tokens, mixer_gain.astype(jnp.float32))
    grad_tokens, grad_mixer_gain = front_pull(grad_normed)
    grad_tokens = grad_tokens + grad_settled
    shard_count = lax.axis_size("ctx") * lax.axis_size("dp")
    big_grads = {
        "front": halved(grad_front, shard_count),
        "outs": jnp.concatenate(
            [halved(grad_ssm_out, shard_count), halved(grad_attn_out, shard_count)], axis=2
        ),
        "gate_up": halved(grad_gate_up, shard_count),
        "ffn_down": halved(grad_down, shard_count),
    }
    small_grads = (
        grad_mixer_gain,
        grad_step_proj,
        grad_taps,
        grad_conv_bias,
        grad_gated_gain,
        grad_ffn_gain,
        grad_bias_a + grad_bias_b,
        grad_log_a + grad_log_b,
        grad_skip,
    )
    return (grad_tokens.reshape(row_count, piece_size, model_width), big_grads, small_grads)


def halved(grad, shard_count):
    rows = grad.shape[0] // (2 * shard_count)
    return grad.astype(jnp.bfloat16).reshape(shard_count, 2, rows, grad.shape[1])


def half_shards(shard, leading):
    rows = shard.shape[0] // 2
    low, high = shard[:rows], shard[rows:]
    received = swapped(jnp.where(leading, high, low), "section", 0)
    return (jnp.where(leading, low, received), jnp.where(leading, received, high))


def gather_whole(half, leading):
    mine = lax.all_gather(half, ("ctx", "dp"))
    other = swapped(mine, "section", 0)
    return jnp.stack(
        [jnp.where(leading, mine, other), jnp.where(leading, other, mine)], axis=1
    )


def scatter_sum(grad, leading):
    low, high = grad[:, 0], grad[:, 1]
    received = swapped(jnp.where(leading, high, low), "section", 0)
    kept = jnp.where(leading, low, high)
    both = (kept.astype(jnp.float32) + received.astype(jnp.float32)).astype(jnp.bfloat16)
    rows = both.shape[1]
    return lax.psum_scatter(
        both.reshape(-1, both.shape[2]), ("ctx", "dp"), scatter_dimension=0, tiled=True
    ).reshape(rows, both.shape[2])


def own_shard(first, second, leading):
    received = swapped(jnp.where(leading, second, first), "section", 0)
    low = jnp.where(leading, first, received)
    high = jnp.where(leading, received, second)
    return (low.astype(jnp.float32), high.astype(jnp.float32))


def on_device(
    block_input,
    out_grad,
    segments,
    mixer_gain,
    mixer_in,
    step_proj,
    step_bias,
    decay_log,
    skip_gain,
    conv_taps,
    conv_bias,
    gated_gain,
    ssm_out,
    qkv_proj,
    attn_out,
    ffn_gain,
    gate_up,
    ffn_down,
):
    section_index = lax.axis_index("section")
    leading = section_index == 0
    ctx_index = lax.axis_index("ctx")
    place = ctx_index * lax.axis_size("dp") + lax.axis_index("dp")
    layers = segments.shape[0]

    small_parts = (
        mixer_gain[0],
        step_proj[0].reshape(-1),
        conv_taps[0].reshape(-1),
        conv_bias[0],
        gated_gain[0],
        ffn_gain[0],
    )
    small_all = lax.all_gather(
        jnp.concatenate(small_parts), ("section", "ctx", "dp")
    ).reshape(layers, -1, sum(part.size for part in small_parts))
    head_all = lax.all_gather(jnp.stack([step_bias[0], decay_log[0], skip_gain[0]]), "section")
    sent = {
        "front": half_shards(jnp.concatenate([mixer_in[0], qkv_proj[0]], axis=1), leading),
        "ssm_out": half_shards(ssm_out[0], leading),
        "attn_out": half_shards(attn_out[0], leading),
        "gate_up": half_shards(gate_up[0], leading),
        "ffn_down": half_shards(ffn_down[0], leading),
    }
    ssm_half = ssm_out.shape[1] // 2
    model_width = ffn_down.shape[2]

    def layer_weights(layer):
        pieces = []
        start = 0
        for part in small_parts:
            pieces.append(small_all[layer, :, start : start + part.size])
            start += part.size
        tap_count = conv_taps.shape[1]
        taps = jnp.transpose(
            pieces[2].reshape(-1, tap_count, conv_taps.shape[2]), (1, 0, 2)
        ).reshape(tap_count, -1)
        small = (
            pieces[0].reshape(-1),
            pieces[1].reshape(-1, step_proj.shape[2]),
            taps,
            pieces[3].reshape(-1),
            pieces[4].reshape(-1),
            pieces[5].reshape(-1),
        )
        front = gather_whole(sent["front"][layer], leading)
        outs = gather_whole(
            jnp.concatenate([sent["ssm_out"][layer], sent["attn_out"][layer]], axis=0), leading
        )
        gate_up_all = gather_whole(sent["gate_up"][layer], leading)
        ffn_down_all = gather_whole(sent["ffn_down"][layer], leading)
        return {
            "small": small,
            "front": front.reshape(-1, front.shape[-1]),
            "ssm_out": outs[:, :, :ssm_half].reshape(-1, model_width),
            "attn_out": outs[:, :, ssm_half:].reshape(-1, model_width),
            "gate_up": gate_up_all.reshape(-1, gate_up_all.shape[-1]),
            "ffn_down": ffn_down_all.reshape(-1, model_width),
        }

    seg_rows = lax.dynamic_index_in_dim(segments, section_index, 0, keepdims=False)
    weights = [layer_weights(layer) for layer in range(layers)]
    hidden = block_input[0]
    kept_states = []
    for layer in range(layers):
        head_params = (head_all[layer, 0], head_all[layer, 1], head_all[layer, 2])
        leaving, saved = layer_forward(
            hidden.astype(jnp.float32), seg_rows, weights[layer], head_params, ctx_index
        )
        hidden = leaving.astype(jnp.bfloat16)
        kept_states.append(saved)
    block_output = hidden
    grad_low = out_grad[0]
    halves = [None] * layers
    small_sums = [None] * layers
    for layer in range(layers - 1, -1, -1):
        head_params = (head_all[layer, 0], head_all[layer, 1], head_all[layer, 2])
        grad_entry, big_grads, small_grads = layer_backward(
            grad_low.astype(jnp.float32), kept_states[layer], weights[layer], head_params
        )
        grad_low = grad_entry.astype(jnp.bfloat16)
        halves[layer] = {name: scatter_sum(grad, leading) for name, grad in big_grads.items()}
        small_sums[layer] = small_grads
    shapes = [grad.shape for grad in small_sums[0]]
    flat = jnp.stack(
        [jnp.concatenate([grad.reshape(-1) for grad in grads]) for grads in small_sums]
    )
    summed = lax.psum(flat, ("section", "ctx", "dp"))
    mine = lax.dynamic_index_in_dim(summed, section_index, 0, keepdims=False)
    small = []
    start = 0
    for shape in shapes:
        size = 1
        for extent in shape:
            size *= extent
        small.append(mine[start : start + size].reshape(shape))
        start += size

    def own_part(array, like, axis):
        extent = like.shape[axis + 1]
        return lax.dynamic_slice_in_dim(array, place * extent, extent, axis)

    owned = {
        name: own_shard(halves[0][name], halves[1][name], leading) for name in halves[0]
    }
    front_grad = jnp.concatenate(owned["front"], axis=0)
    split = mixer_in.shape[2]
    outs_low, outs_high = owned["outs"]
    return (
        block_output[None],
        grad_low[None],
        own_part(small[0], mixer_gain, 0)[None],
        front_grad[:, :split][None],
        own_part(small[1], step_proj, 0)[None],
        small[6][None],
        small[7][None],
        small[8][None],
        own_part(small[2], conv_taps, 1)[None],
        own_part(small[3], conv_bias, 0)[None],
        own_part(small[4], gated_gain, 0)[None],
        jnp.concatenate([outs_low[:ssm_half], outs_high[:ssm_half]], axis=0)[None],
        front_grad[:, split:][None],
        jnp.concatenate([outs_low[ssm_half:], outs_high[ssm_half:]], axis=0)[None],
        own_part(small[5], ffn_gain, 0)[None],
        jnp.concatenate(owned["gate_up"], axis=0)[None],
        jnp.concatenate(owned["ffn_down"], axis=0)[None],
    )


def solution(mesh):
    placed = (
        P("section", "dp", "ctx", None),
        P("section", "dp", "ctx", None),
        P(None, "dp", None),
        P("section", ("ctx", "dp")),
        P("section", ("ctx", "dp"), None),
        P("section", ("ctx", "dp"), None),
        P("section", None),
        P("section", None),
        P("section", None),
        P("section", None, ("ctx", "dp")),
        P("section", ("ctx", "dp")),
        P("section", ("ctx", "dp")),
        P("section", ("ctx", "dp"), None),
        P("section", ("ctx", "dp"), None),
        P("section", ("ctx", "dp"), None),
        P("section", ("ctx", "dp")),
        P("section", ("ctx", "dp"), None),
        P("section", ("ctx", "dp"), None),
    )
    return jax.shard_map(
        on_device,
        mesh=mesh,
        in_specs=placed,
        out_specs=(
            P("section", "dp", "ctx", None),
            P("section", "dp", "ctx", None),
            P("section", ("ctx", "dp")),
            P("section", ("ctx", "dp"), None),
            P("section", ("ctx", "dp"), None),
            P("section", None),
            P("section", None),
            P("section", None),
            P("section", None, ("ctx", "dp")),
            P("section", ("ctx", "dp")),
            P("section", ("ctx", "dp")),
            P("section", ("ctx", "dp"), None),
            P("section", ("ctx", "dp"), None),
            P("section", ("ctx", "dp"), None),
            P("section", ("ctx", "dp")),
            P("section", ("ctx", "dp"), None),
            P("section", ("ctx", "dp"), None),
        ),
        check_vma=False,
    )
```
